32 devices in a mesh: row: 4 (over x, core), col: 8 (over z, y).
Axes of the slice: x: 2, y: 2, z: 4, core: 2. Of those that a mesh axis runs over, the one named last changes fastest.
Arguments:
- strain_rate: bfloat16 [512, 64, 1024], P(('row', 'col')), may hold values from -200 to 200
Outputs:
- cross_spectra: bfloat16 [2, 4, 8, 4, 16, 512], P(None, None, 'col', None, None, 'row')
The draws below stay inside these ranges and needn't reach their ends.
All inputs are finite; a program needn't handle non-finite values.
Results may differ from the reference program's by a relative error of at most 0.0064.
Values may be sent and summed in bfloat16 or wider, within the bound.
No kernel may reach another device: no remote copies, remote signals or barrier semaphores. Data moves between devices by JAX's collectives and lax.ppermute only.
A program may use at most 64 MiB of HBM per device.

```python
import math
import jax
import jax.numpy as jnp
import numpy as np
from jax import lax

CH_DEV = 16
C = 512
W = 64
NS = 1024
HALF = 64
K0 = 6
FS = 4
SMOOTH = 4
N_ROW = 4
N_COL = 8


def draw_strain_rate(key, part):
    keys = jax.random.split(key, 3)
    position = jnp.arange(C, dtype=jnp.float32) / C
    jitter = jax.random.uniform(keys[0], (C,), jnp.float32, -0.35, 0.35)
    window_scale = jnp.exp(jax.random.uniform(keys[1], (W,), jnp.float32, -0.7, 0.7))
    channel_scale = jnp.exp(math.log(10.0) * position + jitter)
    noise = jnp.clip(jax.random.normal(keys[2], (C, W, NS), jnp.float32), -6.0, 6.0)
    values = channel_scale[:, None, None] * window_scale[None, :, None] * noise
    return jnp.clip(values, -200.0, 200.0).astype(jnp.bfloat16)


def setup_inputs(seed: int = 0) -> dict:
    key_of = jax.random.split(jax.random.key(seed), 2)
    strain_rate = draw_strain_rate(jax.random.fold_in(key_of[1], 71), 0)
    return {"strain_rate": strain_rate}


def dft_table():
    sample_index = jnp.arange(NS, dtype=jnp.int32)
    bin_index = K0 + jnp.arange(FS + 2 * SMOOTH, dtype=jnp.int32)
    phases = (sample_index[:, None] * bin_index[None, :] % NS).astype(jnp.float32) * (2.0 * math.pi / NS)
    return jnp.concatenate([jnp.cos(phases), -jnp.sin(phases)], axis=1) / math.sqrt(NS)

def whiten(spectrum):
    bands = FS + 2 * SMOOTH
    real_part = spectrum[..., :bands]
    imag_part = spectrum[..., bands:]
    magnitude = jnp.sqrt(real_part * real_part + imag_part * imag_part)
    smoothed = magnitude[..., 0:FS]
    for offset in range(1, 2 * SMOOTH + 1):
        smoothed = smoothed + magnitude[..., offset:offset + FS]
    divisor = jnp.maximum(smoothed / (2 * SMOOTH + 1), 0.6)
    white_real = real_part[..., SMOOTH:SMOOTH + FS] / divisor
    white_imag = imag_part[..., SMOOTH:SMOOTH + FS] / divisor
    return jnp.stack([white_real, white_imag]).astype(jnp.bfloat16).transpose(0, 3, 2, 1)

def prepare_block(window_block):
    channels = window_block.shape[0]
    magnitude = jnp.abs(window_block.astype(jnp.float32))
    prefix = jnp.concatenate([jnp.zeros(magnitude.shape[:-1] + (1,), jnp.float32), jnp.cumsum(magnitude, axis=-1)], axis=-1)
    positions = np.arange(NS)
    upper = np.minimum(positions + HALF, NS - 1)
    lower = np.maximum(positions - HALF, 0)
    counts = jnp.asarray((upper - lower + 1).astype(np.float32))
    running = prefix[..., upper + 1] - prefix[..., lower]
    flattened = window_block.astype(jnp.float32) / (running / counts + 1e-06)
    spectrum = jnp.dot(flattened.reshape(-1, NS), dft_table(), precision=lax.Precision.HIGHEST)
    return whiten(spectrum.reshape(channels, W, -1))

def reference(strain_rate):
    blocks = strain_rate.reshape(N_ROW, C // N_ROW, W, NS)
    block_power = lax.map(lambda window_block: lax.optimization_barrier(jnp.sum(jnp.square(window_block.astype(jnp.float32)), axis=(0, 2))), blocks)
    power = lax.optimization_barrier(jnp.sum(block_power, axis=0)) / (C * NS)
    window_gain = 1.0 / jnp.sqrt(power + 1e-05)
    gain_square = window_gain * window_gain
    spectra = lax.map(prepare_block, blocks)
    spectra = spectra.transpose(1, 2, 3, 0, 4).reshape(2, FS, W, C)
    weighted = (spectra.astype(jnp.float32) * gain_square[None, None, :, None]).astype(jnp.bfloat16)
    outputs = []
    for bin_number in range(FS):
        first_real = spectra[0, bin_number].astype(jnp.float32)
        first_imag = spectra[1, bin_number].astype(jnp.float32)
        second_real = weighted[0, bin_number].astype(jnp.float32)
        second_imag = weighted[1, bin_number].astype(jnp.float32)
        real_sum = jnp.einsum('wb,wa->ba', second_real, first_real) + jnp.einsum('wb,wa->ba', second_imag, first_imag)
        imag_sum = jnp.einsum('wb,wa->ba', second_real, first_imag) - jnp.einsum('wb,wa->ba', second_imag, first_real)
        both = jnp.stack([real_sum, imag_sum]) / W
        both = both.astype(jnp.bfloat16).reshape(2, N_ROW, N_COL, CH_DEV, C).transpose(0, 2, 1, 3, 4)
        outputs.append(both)
    return jnp.stack(outputs, axis=1)
```

```python
import functools
import math

import jax
import jax.numpy as jnp
import numpy as np
from jax import lax
from jax.experimental import pallas as pl
from jax.experimental.pallas import tpu as pltpu
from jax.sharding import PartitionSpec as P

W = 64
NS = 1024
HALF = 64
K0 = 6
FS = 4
SMOOTH = 4
BANDS = FS + 2 * SMOOTH
PAD = 16
TILE = 256
REACH = 128
LANES = 2 * W
POWER_ROWS = 16

BF16 = jnp.bfloat16
F32 = jnp.float32


def sample_counts():
    sample = np.arange(NS)
    return np.minimum(sample + HALF, NS - 1) - np.maximum(sample - HALF, 0) + 1


def band_block():
    source = np.arange(-REACH, TILE + REACH)[:, None]
    return jnp.asarray(np.abs(source - np.arange(TILE)[None, :]) <= HALF, BF16)


def dft_rows():
    phase = np.outer(K0 + np.arange(BANDS), np.arange(NS)) % NS * (2.0 * math.pi / NS)
    scale = sample_counts() / math.sqrt(NS)
    table = np.zeros((2 * PAD, NS), np.float64)
    table[:BANDS] = np.cos(phase) * scale
    table[PAD : PAD + BANDS] = -np.sin(phase) * scale
    high = table.astype(BF16)
    low = (table - high.astype(np.float64)).astype(BF16)
    return jnp.asarray(np.concatenate([high, low], axis=0))


def count_row():
    return jnp.asarray(sample_counts()[None, :] * 1e-06, F32)


def power_kernel(x_ref, out_ref, total):
    step = pl.program_id(0)

    @pl.when(step == 0)
    def _():
        total[...] = jnp.zeros_like(total)

    partial = None
    for channel in range(x_ref.shape[0]):
        for tile in range(NS // 128):
            value = x_ref[channel, :, tile * 128 : (tile + 1) * 128].astype(F32)
            square = value * value
            partial = square if partial is None else partial + square
    total[...] += partial

    @pl.when(step == pl.num_programs(0) - 1)
    def _():
        columns = jnp.transpose(total[...])
        row = jnp.sum(columns, axis=0, keepdims=True)
        out_ref[...] = jnp.broadcast_to(jnp.concatenate([row, row], axis=1), out_ref.shape)


def local_power(strain_rate, block=4):
    channels = strain_rate.shape[0]
    return pl.pallas_call(
        power_kernel,
        grid=(channels // block,),
        in_specs=[pl.BlockSpec((block, W, NS), lambda i: (i, 0, 0))],
        out_specs=pl.BlockSpec((8, LANES), lambda i: (0, 0)),
        out_shape=jax.ShapeDtypeStruct((8, LANES), F32),
        scratch_shapes=[pltpu.VMEM((W, 128), F32)],
        compiler_params=pltpu.CompilerParams(vmem_limit_bytes=8 * 2**20),
        name="power",
    )(strain_rate)


def whiten_rows(spectrum):
    real_part = spectrum[:BANDS]
    imag_part = spectrum[PAD : PAD + BANDS]
    magnitude = jnp.sqrt(real_part * real_part + imag_part * imag_part)
    smoothed = magnitude[0:FS]
    for offset in range(1, 2 * SMOOTH + 1):
        smoothed = smoothed + magnitude[offset : offset + FS]
    divisor = jnp.maximum(smoothed * (1.0 / (2 * SMOOTH + 1)), 0.6)
    return real_part[SMOOTH : SMOOTH + FS] / divisor, imag_part[SMOOTH : SMOOTH + FS] / divisor


def spectra_kernel(x_ref, band_ref, dft_ref, count_ref, out_ref, rows):
    step = pl.program_id(0)
    block = x_ref.shape[0]
    x = x_ref[...].reshape(block * W, NS)
    magnitude = jnp.abs(x)
    spectrum = None
    for tile in range(NS // TILE):
        start, stop = tile * TILE, (tile + 1) * TILE
        low, high = max(start - REACH, 0), min(stop + REACH, NS)
        skip = low - (start - REACH)
        running = jnp.dot(
            magnitude[:, low:high],
            band_ref[skip : skip + high - low, :],
            preferred_element_type=F32,
        )
        flat = x[:, start:stop].astype(F32) / (running + count_ref[:, start:stop])
        flat_high = flat.astype(BF16)
        flat_low = (flat - flat_high.astype(F32)).astype(BF16)
        dims = (((1,), (1,)), ((), ()))
        both = lax.dot_general(
            dft_ref[:, start:stop], flat_high, dims, preferred_element_type=F32
        )
        rest = lax.dot_general(
            dft_ref[: 2 * PAD, start:stop], flat_low, dims, preferred_element_type=F32
        )
        term = both[: 2 * PAD] + (both[2 * PAD :] + rest)
        spectrum = term if spectrum is None else spectrum + term
    white_real, white_imag = whiten_rows(spectrum)
    first_half = lax.broadcasted_iota(jnp.int32, (FS, LANES), 1) < W
    for pair in range(block // 2):
        real = white_real[:, pair * LANES : (pair + 1) * LANES]
        imag = white_imag[:, pair * LANES : (pair + 1) * LANES]
        even = jnp.where(first_half, real, pltpu.roll(imag, W, 1))
        odd = jnp.where(first_half, pltpu.roll(real, W, 1), imag)
        for bin_number in range(FS):
            channel = step * block + 2 * pair
            rows[bin_number, pl.ds(channel, 1), :] = even[bin_number : bin_number + 1]
            rows[bin_number, pl.ds(channel + 1, 1), :] = odd[bin_number : bin_number + 1]

    @pl.when(step == pl.num_programs(0) - 1)
    def _():
        out_ref[...] = rows[...].astype(BF16)


def local_spectra(strain_rate, block=4):
    channels = strain_rate.shape[0]
    whole = lambda i: (0, 0)
    return pl.pallas_call(
        spectra_kernel,
        grid=(channels // block,),
        in_specs=[
            pl.BlockSpec((block, W, NS), lambda i: (i, 0, 0)),
            pl.BlockSpec((TILE + 2 * REACH, TILE), whole),
            pl.BlockSpec((4 * PAD, NS), whole),
            pl.BlockSpec((1, NS), whole),
        ],
        out_specs=pl.BlockSpec((FS, channels, LANES), lambda i: (0, 0, 0)),
        out_shape=jax.ShapeDtypeStruct((FS, channels, LANES), BF16),
        scratch_shapes=[pltpu.VMEM((FS, channels, LANES), F32)],
        compiler_params=pltpu.CompilerParams(vmem_limit_bytes=40 * 2**20),
        name="spectra",
    )(strain_rate, band_block(), dft_rows(), count_row())


def cross_kernel(order, members, samples, me_ref, gathered_ref, own_ref, *refs):
    *row_refs, out_ref, first, second = refs
    channels = own_ref.shape[1]
    rows = FS * channels
    power = None
    for block in range(len(order)):
        parts = gathered_ref[block, rows : rows + POWER_ROWS, :].astype(F32)
        value = parts[0:1] + (parts[1:2] + parts[2:3])
        power = value if power is None else power + value
    power = power / (channels * members * samples)
    gain = 1.0 / jnp.sqrt(power + 1e-05)
    gain_square = gain * gain
    lane = lax.broadcasted_iota(jnp.int32, (1, LANES), 1)
    turned_gain = jnp.where(lane < W, -gain_square, gain_square)
    me = me_ref[0]
    for shift, ref in enumerate((own_ref, *row_refs)):
        row = jnp.bitwise_xor(me, shift)
        place = pl.ds(pl.multiple_of(row * channels, channels), channels)
        for bin_number in range(FS):
            value = ref[bin_number].astype(F32)
            second[0, bin_number, place, :] = (value * gain_square).astype(BF16)
            second[1, bin_number, place, :] = (pltpu.roll(value, W, 1) * turned_gain).astype(BF16)
    for block, column in enumerate(order):
        for bin_number in range(FS):
            first[bin_number, column * channels : (column + 1) * channels, :] = gathered_ref[
                block, bin_number * channels : (bin_number + 1) * channels, :
            ]
    for bin_number in range(FS):
        for part in range(2):
            total = lax.dot_general(
                second[part, bin_number],
                first[bin_number],
                (((1,), (1,)), ((), ())),
                preferred_element_type=F32,
            )
            out_ref[part, bin_number] = (total * (1.0 / W)).astype(BF16)


def column_order(col_count):
    best = [4, 0, 5, 6, 1, 2, 7, 3]
    if col_count == len(best):
        return best
    middle = col_count // 2
    return [middle, *(c for c in range(col_count) if c != middle)]


def split_three(value):
    high = lax.reduce_precision(value, 8, 7)
    rest = value - high
    middle = lax.reduce_precision(rest, 8, 7)
    return high.astype(BF16), middle.astype(BF16), (rest - middle).astype(BF16)


def shards(strain_rate):
    channels, windows, samples = strain_rate.shape
    row_count = lax.axis_size("row")
    col_count = lax.axis_size("col")
    order = column_order(col_count)

    def from_row(value, shift):
        return lax.ppermute(value, "row", [(i, i ^ shift) for i in range(row_count)])

    own_power = local_power(strain_rate)
    row_power = own_power
    for shift in range(1, row_count):
        row_power = row_power + from_row(own_power, shift)
    spectra = local_spectra(strain_rate)
    power_rows = jnp.concatenate(
        [part[:1] for part in split_three(row_power)]
        + [jnp.zeros((POWER_ROWS - 3, LANES), BF16)],
        axis=0,
    )
    message = jnp.concatenate([spectra.reshape(FS * channels, LANES), power_rows], axis=0)
    gathered = lax.all_to_all(
        jnp.broadcast_to(message, (col_count, *message.shape)), "col", 0, 0, axis_index_groups=[order]
    )
    others = [from_row(spectra, shift) for shift in range(1, row_count)]
    me = lax.axis_index("row").astype(jnp.int32).reshape(1)
    result = pl.pallas_call(
        functools.partial(cross_kernel, order, row_count * col_count, samples),
        in_specs=[pl.BlockSpec(memory_space=pltpu.SMEM)]
        + [pl.BlockSpec(memory_space=pltpu.VMEM)] * (2 + len(others)),
        out_specs=pl.BlockSpec(memory_space=pltpu.VMEM),
        out_shape=jax.ShapeDtypeStruct(
            (2, FS, row_count * channels, col_count * channels), BF16
        ),
        scratch_shapes=[
            pltpu.VMEM((FS, col_count * channels, LANES), BF16),
            pltpu.VMEM((2, FS, row_count * channels, LANES), BF16),
        ],
        compiler_params=pltpu.CompilerParams(vmem_limit_bytes=8 * 2**20),
        name="cross",
    )(me, gathered, spectra, *others)
    return result.reshape(2, FS, 1, row_count, channels, -1)


def solution(mesh):
    return jax.shard_map(
        shards,
        mesh=mesh,
        in_specs=(P(("row", "col"), None, None),),
        out_specs=P(None, None, "col", None, None, "row"),
        check_vma=False,
    )
```

```python
import functools
import math

import jax
import jax.numpy as jnp
from jax import lax
from jax.experimental import pallas as pl
from jax.experimental.pallas import tpu as pltpu
from jax.sharding import PartitionSpec as P

W = 64
NS = 1024
HALF = 64
K0 = 6
FS = 4
SMOOTH = 4
BANDS = FS + 2 * SMOOTH
PAD = 16
TILE = 256
REACH = 128
LANES = 2 * W
POWER_ROWS = 16

BF16 = jnp.bfloat16
F32 = jnp.float32


def power_kernel(x_ref, out_ref):
    def add(channel, total):
        for tile in range(NS // 128):
            value = x_ref[channel, :, tile * 128 : (tile + 1) * 128].astype(F32)
            total = total + value * value
        return total

    total = lax.fori_loop(0, x_ref.shape[0], add, jnp.zeros((W, 128), F32))
    row = jnp.sum(jnp.transpose(total), axis=0, keepdims=True)
    out_ref[...] = jnp.broadcast_to(jnp.concatenate([row, row], axis=1), out_ref.shape)


def in_vmem(count):
    return [pl.BlockSpec(memory_space=pltpu.VMEM)] * count


def local_power(strain_rate):
    return pl.pallas_call(
        power_kernel,
        in_specs=in_vmem(1),
        out_specs=in_vmem(1)[0],
        out_shape=jax.ShapeDtypeStruct((8, LANES), F32),
        compiler_params=pltpu.CompilerParams(vmem_limit_bytes=4 * 2**20),
        name="power",
    )(strain_rate)


def whiten_rows(spectrum):
    real_part = spectrum[:BANDS]
    imag_part = spectrum[PAD : PAD + BANDS]
    magnitude = jnp.sqrt(real_part * real_part + imag_part * imag_part)
    smoothed = magnitude[0:FS]
    for offset in range(1, 2 * SMOOTH + 1):
        smoothed = smoothed + magnitude[offset : offset + FS]
    divisor = jnp.maximum(smoothed * (1.0 / (2 * SMOOTH + 1)), 0.6)
    return real_part[SMOOTH : SMOOTH + FS] / divisor, imag_part[SMOOTH : SMOOTH + FS] / divisor


def window_counts():
    sample = lax.broadcasted_iota(jnp.int32, (1, NS), 1)
    return (jnp.minimum(sample + HALF, NS - 1) - jnp.maximum(sample - HALF, 0) + 1).astype(F32)


def fill_band(band):
    source = lax.broadcasted_iota(jnp.int32, band.shape, 0) - REACH
    target = lax.broadcasted_iota(jnp.int32, band.shape, 1)
    band[...] = jnp.where(jnp.abs(source - target) <= HALF, 1.0, 0.0).astype(BF16)


def fill_dft(dft):
    bins = K0 + lax.broadcasted_iota(jnp.int32, (PAD, 128), 0)
    sample = lax.broadcasted_iota(jnp.int32, (PAD, 128), 1)
    turn = 2.0 * math.pi / NS
    phase = ((bins * sample) & (NS - 1)).astype(F32) * turn
    step = ((bins * 128) & (NS - 1)).astype(F32) * turn
    cos, sin = jnp.cos(phase), jnp.sin(phase)
    step_cos, step_sin = jnp.cos(step), jnp.sin(step)
    scale = window_counts() * (1.0 / math.sqrt(NS))
    for tile in range(NS // 128):
        place = slice(tile * 128, (tile + 1) * 128)
        for part, value in enumerate((cos * scale[:, place], -sin * scale[:, place])):
            high = value.astype(BF16)
            dft[part * PAD : (part + 1) * PAD, place] = high
            dft[(2 + part) * PAD : (3 + part) * PAD, place] = (value - high.astype(F32)).astype(BF16)
        cos, sin = cos * step_cos - sin * step_sin, sin * step_cos + cos * step_sin


def spectra_kernel(block, x_ref, out_ref, rows, band, dft):
    fill_band(band)
    fill_dft(dft)
    channels = x_ref.shape[0]
    small = window_counts() * 1e-06
    first_half = lax.broadcasted_iota(jnp.int32, (FS, LANES), 1) < W
    contract_samples = (((1,), (1,)), ((), ()))
    units = [
        (channel, tile) for channel in range(0, channels, block) for tile in range(NS // TILE)
    ]

    def running_sum(channel, tile):
        start, stop = tile * TILE, (tile + 1) * TILE
        low, high = max(start - REACH, 0), min(stop + REACH, NS)
        skip = low - (start - REACH)
        magnitude = jnp.abs(x_ref[channel : channel + block, :, low:high].reshape(-1, high - low))
        return jnp.dot(
            magnitude, band[skip : skip + high - low, :], preferred_element_type=F32
        )

    def flatten(channel, tile, running):
        start, stop = tile * TILE, (tile + 1) * TILE
        x = x_ref[channel : channel + block, :, start:stop].reshape(-1, TILE).astype(F32)
        flat = x / (running + small[:, start:stop])
        high = flat.astype(BF16)
        return high, (flat - high.astype(F32)).astype(BF16)

    def transform(tile, high, low):
        place = slice(tile * TILE, (tile + 1) * TILE)
        both = lax.dot_general(
            dft[:, place], high, contract_samples, preferred_element_type=F32
        )
        rest = lax.dot_general(
            dft[: 2 * PAD, place], low, contract_samples, preferred_element_type=F32
        )
        return both[: 2 * PAD] + (both[2 * PAD :] + rest)

    def store(channel, spectrum):
        white_real, white_imag = whiten_rows(spectrum)
        for pair in range(block // 2):
            real = white_real[:, pair * LANES : (pair + 1) * LANES]
            imag = white_imag[:, pair * LANES : (pair + 1) * LANES]
            even = jnp.where(first_half, real, pltpu.roll(imag, W, 1))
            odd = jnp.where(first_half, pltpu.roll(real, W, 1), imag)
            for bin_number in range(FS):
                for offset, value in enumerate((even, odd)):
                    row = channel + 2 * pair + offset
                    rows[bin_number, row : row + 1, :] = value[bin_number : bin_number + 1]

    spectrum = None
    running = running_sum(*units[0])
    for index, (channel, tile) in enumerate(units):
        following = running_sum(*units[index + 1]) if index + 1 < len(units) else None
        term = transform(tile, *flatten(channel, tile, running))
        spectrum = term if tile == 0 else spectrum + term
        if tile == NS // TILE - 1:
            store(channel, spectrum)
        running = following
    out_ref[...] = rows[...].astype(BF16)


def local_spectra(strain_rate, block=8):
    channels = strain_rate.shape[0]
    return pl.pallas_call(
        functools.partial(spectra_kernel, block),
        in_specs=in_vmem(1),
        out_specs=in_vmem(1)[0],
        out_shape=jax.ShapeDtypeStruct((FS, channels, LANES), BF16),
        scratch_shapes=[
            pltpu.VMEM((FS, channels, LANES), F32),
            pltpu.VMEM((TILE + 2 * REACH, TILE), BF16),
            pltpu.VMEM((4 * PAD, NS), BF16),
        ],
        compiler_params=pltpu.CompilerParams(vmem_limit_bytes=24 * 2**20),
        name="spectra",
    )(strain_rate)


def message_kernel(spectra_ref, own_ref, *refs):
    *power_refs, out_ref = refs
    rows = spectra_ref.shape[0] * spectra_ref.shape[1]
    power = own_ref[...]
    for ref in power_refs:
        power = power + ref[...]
    high = power.astype(BF16)
    rest = power - high.astype(F32)
    middle = rest.astype(BF16)
    low = (rest - middle.astype(F32)).astype(BF16)
    line = lax.broadcasted_iota(jnp.int32, power.shape, 0)
    parts = jnp.where(
        line == 0, high.astype(F32), jnp.where(line == 1, middle.astype(F32), low.astype(F32))
    )
    power_rows = jnp.concatenate([parts, parts], axis=0).astype(BF16)
    spectra = spectra_ref[...].reshape(rows, LANES)
    for receiver in range(out_ref.shape[0]):
        out_ref[receiver, :rows, :] = spectra
        out_ref[receiver, rows:, :] = power_rows


def cross_kernel(order, members, samples, me_ref, gathered_ref, own_ref, *refs):
    *row_refs, out_ref, first, second = refs
    channels = own_ref.shape[1]
    rows = FS * channels
    power = None
    for block in range(len(order)):
        parts = gathered_ref[block, rows : rows + POWER_ROWS, :].astype(F32)
        value = parts[0:1] + (parts[1:2] + parts[2:3])
        power = value if power is None else power + value
    power = power / (channels * members * samples)
    gain = 1.0 / jnp.sqrt(power + 1e-05)
    gain_square = gain * gain
    lane = lax.broadcasted_iota(jnp.int32, (1, LANES), 1)
    turned_gain = jnp.where(lane < W, -gain_square, gain_square)
    me = me_ref[0]
    for shift, ref in enumerate((own_ref, *row_refs)):
        row = jnp.bitwise_xor(me, shift)
        place = pl.ds(pl.multiple_of(row * channels, channels), channels)
        for bin_number in range(FS):
            value = ref[bin_number].astype(F32)
            second[0, bin_number, place, :] = (value * gain_square).astype(BF16)
            second[1, bin_number, place, :] = (pltpu.roll(value, W, 1) * turned_gain).astype(BF16)
    for block, column in enumerate(order):
        for bin_number in range(FS):
            first[bin_number, column * channels : (column + 1) * channels, :] = gathered_ref[
                block, bin_number * channels : (bin_number + 1) * channels, :
            ]
    for bin_number in range(FS):
        for part in range(2):
            total = lax.dot_general(
                second[part, bin_number],
                first[bin_number],
                (((1,), (1,)), ((), ())),
                preferred_element_type=F32,
            )
            out_ref[part, bin_number] = (total * (1.0 / W)).astype(BF16)


def column_order(col_count):
    best = [4, 0, 5, 6, 1, 2, 7, 3]
    if col_count == len(best):
        return best
    middle = col_count // 2
    return [middle, *(c for c in range(col_count) if c != middle)]


def shards(strain_rate):
    channels, windows, samples = strain_rate.shape
    row_count = lax.axis_size("row")
    col_count = lax.axis_size("col")
    order = column_order(col_count)

    def from_row(value, shift):
        return lax.ppermute(value, "row", [(i, i ^ shift) for i in range(row_count)])

    own_power = local_power(strain_rate)
    powers = [from_row(own_power, shift) for shift in range(1, row_count)]
    spectra = local_spectra(strain_rate)
    message = pl.pallas_call(
        message_kernel,
        in_specs=in_vmem(1 + row_count),
        out_specs=in_vmem(1)[0],
        out_shape=jax.ShapeDtypeStruct((col_count, FS * channels + POWER_ROWS, LANES), BF16),
        compiler_params=pltpu.CompilerParams(vmem_limit_bytes=8 * 2**20),
        name="message",
    )(spectra, own_power, *powers)
    gathered = lax.all_to_all(message, "col", 0, 0, axis_index_groups=[order])
    others = [from_row(spectra, shift) for shift in range(1, row_count)]
    me = lax.axis_index("row").astype(jnp.int32).reshape(1)
    result = pl.pallas_call(
        functools.partial(cross_kernel, order, row_count * col_count, samples),
        in_specs=[pl.BlockSpec(memory_space=pltpu.SMEM)]
        + [pl.BlockSpec(memory_space=pltpu.VMEM)] * (2 + len(others)),
        out_specs=pl.BlockSpec(memory_space=pltpu.VMEM),
        out_shape=jax.ShapeDtypeStruct(
            (2, FS, row_count * channels, col_count * channels), BF16
        ),
        scratch_shapes=[
            pltpu.VMEM((FS, col_count * channels, LANES), BF16),
            pltpu.VMEM((2, FS, row_count * channels, LANES), BF16),
        ],
        compiler_params=pltpu.CompilerParams(vmem_limit_bytes=8 * 2**20),
        name="cross",
    )(me, gathered, spectra, *others)
    return result.reshape(2, FS, 1, row_count, channels, -1)


def solution(mesh):
    return jax.shard_map(
        shards,
        mesh=mesh,
        in_specs=(P(("row", "col"), None, None),),
        out_specs=P(None, None, "col", None, None, "row"),
        check_vma=False,
    )
```

```python
import functools
import math

import jax
import jax.numpy as jnp
from jax import lax
from jax.experimental import pallas as pl
from jax.experimental.pallas import tpu as pltpu
from jax.sharding import PartitionSpec as P

W = 64
NS = 1024
HALF = 64
K0 = 6
FS = 4
SMOOTH = 4
BANDS = FS + 2 * SMOOTH
PAD = 16
TILE = 256
REACH = 128
LANES = 2 * W
POWER_ROWS = 16

BF16 = jnp.bfloat16
F32 = jnp.float32


def in_vmem(count):
    return [pl.BlockSpec(memory_space=pltpu.VMEM)] * count


def whiten_rows(spectrum):
    real_part = spectrum[:BANDS]
    imag_part = spectrum[PAD : PAD + BANDS]
    magnitude = jnp.sqrt(real_part * real_part + imag_part * imag_part)
    smoothed = magnitude[0:FS]
    for offset in range(1, 2 * SMOOTH + 1):
        smoothed = smoothed + magnitude[offset : offset + FS]
    divisor = jnp.maximum(smoothed * (1.0 / (2 * SMOOTH + 1)), 0.6)
    return real_part[SMOOTH : SMOOTH + FS] / divisor, imag_part[SMOOTH : SMOOTH + FS] / divisor


def window_counts():
    sample = lax.broadcasted_iota(jnp.int32, (1, NS), 1)
    return (jnp.minimum(sample + HALF, NS - 1) - jnp.maximum(sample - HALF, 0) + 1).astype(F32)


def fill_band(band):
    source = lax.broadcasted_iota(jnp.int32, band.shape, 0) - REACH
    target = lax.broadcasted_iota(jnp.int32, band.shape, 1)
    band[...] = jnp.where(jnp.abs(source - target) <= HALF, 1.0, 0.0).astype(BF16)


def fill_dft(dft):
    bins = K0 + lax.broadcasted_iota(jnp.int32, (PAD, 128), 0)
    sample = lax.broadcasted_iota(jnp.int32, (PAD, 128), 1)
    turn = 2.0 * math.pi / NS
    phase = ((bins * sample) & (NS - 1)).astype(F32) * turn
    step = ((bins * 128) & (NS - 1)).astype(F32) * turn
    cos, sin = jnp.cos(phase), jnp.sin(phase)
    step_cos, step_sin = jnp.cos(step), jnp.sin(step)
    scale = window_counts() * (1.0 / math.sqrt(NS))
    for tile in range(NS // 128):
        place = slice(tile * 128, (tile + 1) * 128)
        for part, value in enumerate((cos * scale[:, place], -sin * scale[:, place])):
            high = value.astype(BF16)
            dft[part * PAD : (part + 1) * PAD, place] = high
            dft[(2 + part) * PAD : (3 + part) * PAD, place] = (value - high.astype(F32)).astype(BF16)
        cos, sin = cos * step_cos - sin * step_sin, sin * step_cos + cos * step_sin


def front_kernel(x_hbm, x_ref, power_ref, band, dft, arrived):
    parts = arrived.shape[0]
    size = x_hbm.shape[0] // parts
    copies = [
        pltpu.make_async_copy(
            x_hbm.at[pl.ds(part * size, size)], x_ref.at[pl.ds(part * size, size)], arrived.at[part]
        )
        for part in range(parts)
    ]
    for copy in copies:
        copy.start()
    fill_band(band)
    fill_dft(dft)
    total = jnp.zeros((W, 128), F32)
    for part, copy in enumerate(copies):
        copy.wait()
        for channel in range(part * size, (part + 1) * size):
            for tile in range(NS // 128):
                value = x_ref[channel, :, tile * 128 : (tile + 1) * 128].astype(F32)
                total = total + value * value
    row = jnp.sum(jnp.transpose(total), axis=0, keepdims=True)
    power_ref[...] = jnp.broadcast_to(jnp.concatenate([row, row], axis=1), power_ref.shape)


def front(strain_rate, parts=8):
    return pl.pallas_call(
        front_kernel,
        in_specs=[pl.BlockSpec(memory_space=pltpu.HBM)],
        out_specs=in_vmem(4),
        out_shape=[
            jax.ShapeDtypeStruct(strain_rate.shape, BF16),
            jax.ShapeDtypeStruct((8, LANES), F32),
            jax.ShapeDtypeStruct((TILE + 2 * REACH, TILE), BF16),
            jax.ShapeDtypeStruct((4 * PAD, NS), BF16),
        ],
        scratch_shapes=[pltpu.SemaphoreType.DMA((math.gcd(parts, strain_rate.shape[0]),))],
        compiler_params=pltpu.CompilerParams(vmem_limit_bytes=51 * 2**20),
        name="front",
    )(strain_rate)


def spectra_kernel(block, x_ref, band, dft, out_ref, rows):
    channels = x_ref.shape[0]
    small = window_counts() * 1e-06
    first_half = lax.broadcasted_iota(jnp.int32, (FS, LANES), 1) < W
    contract_samples = (((1,), (1,)), ((), ()))
    units = [
        (channel, tile) for channel in range(0, channels, block) for tile in range(NS // TILE)
    ]

    def running_sum(channel, tile):
        start, stop = tile * TILE, (tile + 1) * TILE
        low, high = max(start - REACH, 0), min(stop + REACH, NS)
        skip = low - (start - REACH)
        magnitude = jnp.abs(x_ref[channel : channel + block, :, low:high].reshape(-1, high - low))
        return jnp.dot(
            magnitude, band[skip : skip + high - low, :], preferred_element_type=F32
        )

    def flatten(channel, tile, running):
        start, stop = tile * TILE, (tile + 1) * TILE
        x = x_ref[channel : channel + block, :, start:stop].reshape(-1, TILE).astype(F32)
        flat = x / (running + small[:, start:stop])
        high = flat.astype(BF16)
        return high, (flat - high.astype(F32)).astype(BF16)

    def transform(tile, high, low):
        place = slice(tile * TILE, (tile + 1) * TILE)
        both = lax.dot_general(
            dft[:, place], high, contract_samples, preferred_element_type=F32
        )
        rest = lax.dot_general(
            dft[: 2 * PAD, place], low, contract_samples, preferred_element_type=F32
        )
        return both[: 2 * PAD] + (both[2 * PAD :] + rest)

    def store(channel, spectrum):
        white_real, white_imag = whiten_rows(spectrum)
        for pair in range(block // 2):
            real = white_real[:, pair * LANES : (pair + 1) * LANES]
            imag = white_imag[:, pair * LANES : (pair + 1) * LANES]
            even = jnp.where(first_half, real, pltpu.roll(imag, W, 1))
            odd = jnp.where(first_half, pltpu.roll(real, W, 1), imag)
            for bin_number in range(FS):
                for offset, value in enumerate((even, odd)):
                    row = channel + 2 * pair + offset
                    rows[bin_number, row : row + 1, :] = value[bin_number : bin_number + 1]

    summed, flattened = {}, {}
    for index in range(len(units) + 2):
        if index < len(units):
            summed[index] = running_sum(*units[index])
        if 1 <= index <= len(units):
            flattened[index - 1] = flatten(*units[index - 1], summed.pop(index - 1))
        if index >= 2:
            channel, tile = units[index - 2]
            term = transform(tile, *flattened.pop(index - 2))
            spectrum = term if tile == 0 else spectrum + term
            if tile == NS // TILE - 1:
                store(channel, spectrum)
    out_ref[...] = rows[...].astype(BF16)


def local_spectra(strain_rate, band, dft, block=8):
    channels = strain_rate.shape[0]
    return pl.pallas_call(
        functools.partial(spectra_kernel, block),
        in_specs=in_vmem(3),
        out_specs=in_vmem(1)[0],
        out_shape=jax.ShapeDtypeStruct((FS, channels, LANES), BF16),
        scratch_shapes=[pltpu.VMEM((FS, channels, LANES), F32)],
        compiler_params=pltpu.CompilerParams(vmem_limit_bytes=24 * 2**20),
        name="spectra",
    )(strain_rate, band, dft)


def message_kernel(spectra_ref, own_ref, *refs):
    *power_refs, out_ref = refs
    rows = spectra_ref.shape[0] * spectra_ref.shape[1]
    power = own_ref[...]
    for ref in power_refs:
        power = power + ref[...]
    high = power.astype(BF16)
    rest = power - high.astype(F32)
    middle = rest.astype(BF16)
    low = (rest - middle.astype(F32)).astype(BF16)
    line = lax.broadcasted_iota(jnp.int32, power.shape, 0)
    parts = jnp.where(
        line == 0, high.astype(F32), jnp.where(line == 1, middle.astype(F32), low.astype(F32))
    )
    power_rows = jnp.concatenate([parts, parts], axis=0).astype(BF16)
    spectra = spectra_ref[...].reshape(rows, LANES)
    for receiver in range(out_ref.shape[0]):
        out_ref[receiver, :rows, :] = spectra
        out_ref[receiver, rows:, :] = power_rows


def cross_kernel(order, members, samples, gathered_ref, own_ref, *refs):
    *row_refs, out_hbm, second, out_ref, sent = refs
    channels = own_ref.shape[1]
    rows = FS * channels
    power = None
    for block in range(len(order)):
        parts = gathered_ref[block, rows : rows + POWER_ROWS, :].astype(F32)
        value = parts[0:1] + (parts[1:2] + parts[2:3])
        power = value if power is None else power + value
    power = power / (channels * members * samples)
    gain = 1.0 / jnp.sqrt(power + 1e-05)
    gain_square = gain * gain
    lane = lax.broadcasted_iota(jnp.int32, (1, LANES), 1)
    turned_gain = jnp.where(lane < W, -gain_square, gain_square)
    me = lax.axis_index("row")
    copies = []
    for bin_number in range(FS):
        for shift, ref in enumerate((own_ref, *row_refs)):
            row = jnp.bitwise_xor(me, shift)
            place = pl.ds(pl.multiple_of(row * channels, channels), channels)
            value = ref[bin_number].astype(F32)
            second[bin_number, 0, place, :] = (value * gain_square).astype(BF16)
            second[bin_number, 1, place, :] = (pltpu.roll(value, W, 1) * turned_gain).astype(BF16)
        first = jnp.concatenate(
            [
                gathered_ref[order.index(column), bin_number * channels : (bin_number + 1) * channels, :]
                for column in range(len(order))
            ],
            axis=0,
        )
        total = lax.dot_general(
            second[bin_number].reshape(-1, LANES),
            first,
            (((1,), (1,)), ((), ())),
            preferred_element_type=F32,
        )
        out_ref[bin_number] = (total * (1.0 / W)).astype(BF16).reshape(out_ref.shape[1:])
        copy = pltpu.make_async_copy(
            out_ref.at[bin_number], out_hbm.at[:, bin_number], sent.at[bin_number]
        )
        copy.start()
        copies.append(copy)
    for copy in copies:
        copy.wait()


def column_order(col_count):
    best = [4, 2, 6, 5, 1, 0, 7, 3]
    if col_count == len(best):
        return best
    middle = col_count // 2
    return [middle, *(c for c in range(col_count) if c != middle)]


def shards(strain_rate):
    channels, windows, samples = strain_rate.shape
    row_count = lax.axis_size("row")
    col_count = lax.axis_size("col")
    order = column_order(col_count)

    def from_row(value, shift):
        return lax.ppermute(value, "row", [(i, i ^ shift) for i in range(row_count)])

    held, own_power, band, dft = front(strain_rate)
    powers = [from_row(own_power, shift) for shift in range(1, row_count)]
    spectra = local_spectra(held, band, dft)
    message = pl.pallas_call(
        message_kernel,
        in_specs=in_vmem(1 + row_count),
        out_specs=in_vmem(1)[0],
        out_shape=jax.ShapeDtypeStruct((col_count, FS * channels + POWER_ROWS, LANES), BF16),
        compiler_params=pltpu.CompilerParams(vmem_limit_bytes=8 * 2**20),
        name="message",
    )(spectra, own_power, *powers)
    gathered = lax.all_to_all(message, "col", 0, 0, axis_index_groups=[order])
    others = [from_row(spectra, shift) for shift in range(1, row_count)]
    result = pl.pallas_call(
        functools.partial(cross_kernel, order, row_count * col_count, samples),
        in_specs=in_vmem(2 + len(others)),
        out_specs=pl.BlockSpec(memory_space=pltpu.HBM),
        out_shape=jax.ShapeDtypeStruct(
            (2, FS, row_count * channels, col_count * channels), BF16
        ),
        scratch_shapes=[
            pltpu.VMEM((FS, 2, row_count * channels, LANES), BF16),
            pltpu.VMEM((FS, 2, row_count * channels, col_count * channels), BF16),
            pltpu.SemaphoreType.DMA((FS,)),
        ],
        compiler_params=pltpu.CompilerParams(vmem_limit_bytes=8 * 2**20),
        name="cross",
    )(gathered, spectra, *others)
    return result.reshape(2, FS, 1, row_count, channels, -1)


def solution(mesh):
    return jax.shard_map(
        shards,
        mesh=mesh,
        in_specs=(P(("row", "col"), None, None),),
        out_specs=P(None, None, "col", None, None, "row"),
        check_vma=False,
    )
```

```python
import functools
import math

import jax
import jax.numpy as jnp
from jax import lax
from jax.experimental import pallas as pl
from jax.experimental.pallas import tpu as pltpu
from jax.sharding import PartitionSpec as P

W = 64
NS = 1024
HALF = 64
K0 = 6
FS = 4
SMOOTH = 4
BANDS = FS + 2 * SMOOTH
PAD = 16
TILE = 256
REACH = 128
LANES = 2 * W
POWER_ROWS = 16

BF16 = jnp.bfloat16
F32 = jnp.float32


def in_vmem(count):
    return [pl.BlockSpec(memory_space=pltpu.VMEM)] * count


def whiten_rows(spectrum):
    real_part = spectrum[:BANDS]
    imag_part = spectrum[PAD : PAD + BANDS]
    magnitude = jnp.sqrt(real_part * real_part + imag_part * imag_part)
    smoothed = magnitude[0:FS]
    for offset in range(1, 2 * SMOOTH + 1):
        smoothed = smoothed + magnitude[offset : offset + FS]
    divisor = jnp.maximum(smoothed * (1.0 / (2 * SMOOTH + 1)), 0.6)
    return real_part[SMOOTH : SMOOTH + FS] / divisor, imag_part[SMOOTH : SMOOTH + FS] / divisor


def window_counts():
    sample = lax.broadcasted_iota(jnp.int32, (1, NS), 1)
    return (jnp.minimum(sample + HALF, NS - 1) - jnp.maximum(sample - HALF, 0) + 1).astype(F32)


def fill_band(band):
    source = lax.broadcasted_iota(jnp.int32, band.shape, 0) - REACH
    target = lax.broadcasted_iota(jnp.int32, band.shape, 1)
    band[...] = jnp.where(jnp.abs(source - target) <= HALF, 1.0, 0.0).astype(BF16)


def fill_dft(dft):
    bins = K0 + lax.broadcasted_iota(jnp.int32, (PAD, 128), 0)
    sample = lax.broadcasted_iota(jnp.int32, (PAD, 128), 1)
    turn = 2.0 * math.pi / NS
    phase = ((bins * sample) & (NS - 1)).astype(F32) * turn
    step = ((bins * 128) & (NS - 1)).astype(F32) * turn
    cos, sin = jnp.cos(phase), jnp.sin(phase)
    step_cos, step_sin = jnp.cos(step), jnp.sin(step)
    scale = window_counts() * (1.0 / math.sqrt(NS))
    for tile in range(NS // 128):
        place = slice(tile * 128, (tile + 1) * 128)
        for part, value in enumerate((cos * scale[:, place], -sin * scale[:, place])):
            high = value.astype(BF16)
            dft[part * PAD : (part + 1) * PAD, place] = high
            dft[(2 + part) * PAD : (3 + part) * PAD, place] = (value - high.astype(F32)).astype(BF16)
        cos, sin = cos * step_cos - sin * step_sin, sin * step_cos + cos * step_sin


def front_kernel(x_hbm, x_ref, power_ref, band, dft, arrived):
    parts = arrived.shape[0]
    size = x_hbm.shape[0] // parts
    copies = [
        pltpu.make_async_copy(
            x_hbm.at[pl.ds(part * size, size)], x_ref.at[pl.ds(part * size, size)], arrived.at[part]
        )
        for part in range(parts)
    ]
    for copy in copies:
        copy.start()
    fill_band(band)
    fill_dft(dft)
    total = jnp.zeros((W, 128), F32)
    for part, copy in enumerate(copies):
        copy.wait()
        for channel in range(part * size, (part + 1) * size):
            for tile in range(NS // 128):
                value = x_ref[channel, :, tile * 128 : (tile + 1) * 128].astype(F32)
                total = total + value * value
    row = jnp.sum(jnp.transpose(total), axis=0, keepdims=True)
    power_ref[...] = jnp.concatenate([row, row], axis=1)


def front(strain_rate, parts=8):
    return pl.pallas_call(
        front_kernel,
        in_specs=[pl.BlockSpec(memory_space=pltpu.HBM)],
        out_specs=in_vmem(4),
        out_shape=[
            jax.ShapeDtypeStruct(strain_rate.shape, BF16),
            jax.ShapeDtypeStruct((1, LANES), F32),
            jax.ShapeDtypeStruct((TILE + 2 * REACH, TILE), BF16),
            jax.ShapeDtypeStruct((4 * PAD, NS), BF16),
        ],
        scratch_shapes=[pltpu.SemaphoreType.DMA((math.gcd(parts, strain_rate.shape[0]),))],
        compiler_params=pltpu.CompilerParams(vmem_limit_bytes=51 * 2**20),
        name="front",
    )(strain_rate)


def spectra_kernel(block, x_ref, band, dft, out_ref, rows):
    channels = x_ref.shape[0]
    small = window_counts() * 1e-06
    first_half = lax.broadcasted_iota(jnp.int32, (FS, LANES), 1) < W
    contract_samples = (((1,), (1,)), ((), ()))
    units = [
        (channel, tile) for channel in range(0, channels, block) for tile in range(NS // TILE)
    ]

    def running_sum(channel, tile):
        start, stop = tile * TILE, (tile + 1) * TILE
        low, high = max(start - REACH, 0), min(stop + REACH, NS)
        skip = low - (start - REACH)
        magnitude = jnp.abs(x_ref[channel : channel + block, :, low:high].reshape(-1, high - low))
        return jnp.dot(
            magnitude, band[skip : skip + high - low, :], preferred_element_type=F32
        )

    def flatten(channel, tile, running):
        start, stop = tile * TILE, (tile + 1) * TILE
        x = x_ref[channel : channel + block, :, start:stop].reshape(-1, TILE).astype(F32)
        flat = x / (running + small[:, start:stop])
        high = flat.astype(BF16)
        return high, (flat - high.astype(F32)).astype(BF16)

    def transform(tile, high, low):
        place = slice(tile * TILE, (tile + 1) * TILE)
        both = lax.dot_general(
            dft[:, place], high, contract_samples, preferred_element_type=F32
        )
        rest = lax.dot_general(
            dft[: 2 * PAD, place], low, contract_samples, preferred_element_type=F32
        )
        return both[: 2 * PAD] + (both[2 * PAD :] + rest)

    def store(channel, spectrum):
        white_real, white_imag = whiten_rows(spectrum)
        for pair in range(block // 2):
            real = white_real[:, pair * LANES : (pair + 1) * LANES]
            imag = white_imag[:, pair * LANES : (pair + 1) * LANES]
            even = jnp.where(first_half, real, pltpu.roll(imag, W, 1))
            odd = jnp.where(first_half, pltpu.roll(real, W, 1), imag)
            for bin_number in range(FS):
                for offset, value in enumerate((even, odd)):
                    row = channel + 2 * pair + offset
                    rows[bin_number, row : row + 1, :] = value[bin_number : bin_number + 1]

    summed, flattened = {}, {}
    for index in range(len(units) + 2):
        if index < len(units):
            summed[index] = running_sum(*units[index])
        if 1 <= index <= len(units):
            flattened[index - 1] = flatten(*units[index - 1], summed.pop(index - 1))
        if index >= 2:
            channel, tile = units[index - 2]
            term = transform(tile, *flattened.pop(index - 2))
            spectrum = term if tile == 0 else spectrum + term
            if tile == NS // TILE - 1:
                store(channel, spectrum)
    out_ref[...] = rows[...].astype(BF16)


def local_spectra(strain_rate, band, dft, block=8):
    channels = strain_rate.shape[0]
    return pl.pallas_call(
        functools.partial(spectra_kernel, block),
        in_specs=in_vmem(3),
        out_specs=in_vmem(1)[0],
        out_shape=jax.ShapeDtypeStruct((FS, channels, LANES), BF16),
        scratch_shapes=[pltpu.VMEM((FS, channels, LANES), F32)],
        compiler_params=pltpu.CompilerParams(vmem_limit_bytes=24 * 2**20),
        name="spectra",
    )(strain_rate, band, dft)


def message_kernel(spectra_ref, own_ref, *refs):
    *power_refs, out_ref = refs
    rows = spectra_ref.shape[0] * spectra_ref.shape[1]
    power = own_ref[...]
    for ref in power_refs:
        power = power + ref[...]
    power = jnp.broadcast_to(power, (8, LANES))
    high = power.astype(BF16)
    rest = power - high.astype(F32)
    middle = rest.astype(BF16)
    low = (rest - middle.astype(F32)).astype(BF16)
    line = lax.broadcasted_iota(jnp.int32, power.shape, 0)
    parts = jnp.where(
        line == 0, high.astype(F32), jnp.where(line == 1, middle.astype(F32), low.astype(F32))
    )
    power_rows = jnp.concatenate([parts, parts], axis=0).astype(BF16)
    spectra = spectra_ref[...].reshape(rows, LANES)
    for receiver in range(out_ref.shape[0]):
        out_ref[receiver, :rows, :] = spectra
        out_ref[receiver, rows:, :] = power_rows


def cross_kernel(order, members, samples, gathered_ref, own_ref, *refs):
    *row_refs, out_hbm, second, out_ref, sent = refs
    channels = own_ref.shape[1]
    rows = FS * channels
    power = None
    for block in range(len(order)):
        parts = gathered_ref[block, rows : rows + POWER_ROWS, :].astype(F32)
        value = parts[0:1] + (parts[1:2] + parts[2:3])
        power = value if power is None else power + value
    power = power / (channels * members * samples)
    gain = 1.0 / jnp.sqrt(power + 1e-05)
    gain_square = gain * gain
    lane = lax.broadcasted_iota(jnp.int32, (1, LANES), 1)
    turned_gain = jnp.where(lane < W, -gain_square, gain_square)
    me = lax.axis_index("row")
    copies = []
    for bin_number in range(FS):
        for shift, ref in enumerate((own_ref, *row_refs)):
            row = jnp.bitwise_xor(me, shift)
            place = pl.ds(pl.multiple_of(row * channels, channels), channels)
            value = ref[bin_number].astype(F32)
            second[bin_number, 0, place, :] = (value * gain_square).astype(BF16)
            second[bin_number, 1, place, :] = (pltpu.roll(value, W, 1) * turned_gain).astype(BF16)
        first = jnp.concatenate(
            [
                gathered_ref[order.index(column), bin_number * channels : (bin_number + 1) * channels, :]
                for column in range(len(order))
            ],
            axis=0,
        )
        total = lax.dot_general(
            second[bin_number].reshape(-1, LANES),
            first,
            (((1,), (1,)), ((), ())),
            preferred_element_type=F32,
        )
        out_ref[bin_number] = (total * (1.0 / W)).astype(BF16).reshape(out_ref.shape[1:])
        copy = pltpu.make_async_copy(
            out_ref.at[bin_number], out_hbm.at[:, bin_number], sent.at[bin_number]
        )
        copy.start()
        copies.append(copy)
    for copy in copies:
        copy.wait()


def column_order(col_count):
    best = [4, 2, 3, 6, 5, 1, 0, 7]
    if col_count == len(best):
        return best
    middle = col_count // 2
    return [middle, *(c for c in range(col_count) if c != middle)]


def shards(strain_rate):
    channels, windows, samples = strain_rate.shape
    row_count = lax.axis_size("row")
    col_count = lax.axis_size("col")
    order = column_order(col_count)

    def from_row(value, shift):
        return lax.ppermute(value, "row", [(i, i ^ shift) for i in range(row_count)])

    held, own_power, band, dft = front(strain_rate)
    powers = [from_row(own_power, shift) for shift in range(1, row_count)]
    spectra = local_spectra(held, band, dft)
    message = pl.pallas_call(
        message_kernel,
        in_specs=in_vmem(1 + row_count),
        out_specs=in_vmem(1)[0],
        out_shape=jax.ShapeDtypeStruct((col_count, FS * channels + POWER_ROWS, LANES), BF16),
        compiler_params=pltpu.CompilerParams(vmem_limit_bytes=8 * 2**20),
        name="message",
    )(spectra, own_power, *powers)
    gathered = lax.all_to_all(message, "col", 0, 0, axis_index_groups=[order])
    others = [from_row(spectra, shift) for shift in range(1, row_count)]
    result = pl.pallas_call(
        functools.partial(cross_kernel, order, row_count * col_count, samples),
        in_specs=in_vmem(2 + len(others)),
        out_specs=pl.BlockSpec(memory_space=pltpu.HBM),
        out_shape=jax.ShapeDtypeStruct(
            (2, FS, row_count * channels, col_count * channels), BF16
        ),
        scratch_shapes=[
            pltpu.VMEM((FS, 2, row_count * channels, LANES), BF16),
            pltpu.VMEM((FS, 2, row_count * channels, col_count * channels), BF16),
            pltpu.SemaphoreType.DMA((FS,)),
        ],
        compiler_params=pltpu.CompilerParams(vmem_limit_bytes=8 * 2**20),
        name="cross",
    )(gathered, spectra, *others)
    return result.reshape(2, FS, 1, row_count, channels, -1)


def solution(mesh):
    return jax.shard_map(
        shards,
        mesh=mesh,
        in_specs=(P(("row", "col"), None, None),),
        out_specs=P(None, None, "col", None, None, "row"),
        check_vma=False,
    )
```

```python
import functools
import math

import jax
import jax.numpy as jnp
from jax import lax
from jax.experimental import pallas as pl
from jax.experimental.pallas import tpu as pltpu
from jax.sharding import PartitionSpec as P

W = 64
NS = 1024
HALF = 64
K0 = 6
FS = 4
SMOOTH = 4
BANDS = FS + 2 * SMOOTH
PAD = 16
TILE = 256
REACH = 128
LANES = 2 * W
POWER_ROWS = 16

BF16 = jnp.bfloat16
F32 = jnp.float32


def in_vmem(count):
    return [pl.BlockSpec(memory_space=pltpu.VMEM)] * count


def whiten_rows(spectrum):
    real_part = spectrum[:BANDS]
    imag_part = spectrum[PAD : PAD + BANDS]
    magnitude = jnp.sqrt(real_part * real_part + imag_part * imag_part)
    smoothed = magnitude[0:FS]
    for offset in range(1, 2 * SMOOTH + 1):
        smoothed = smoothed + magnitude[offset : offset + FS]
    divisor = jnp.maximum(smoothed * (1.0 / (2 * SMOOTH + 1)), 0.6)
    return real_part[SMOOTH : SMOOTH + FS] / divisor, imag_part[SMOOTH : SMOOTH + FS] / divisor


def window_counts():
    sample = lax.broadcasted_iota(jnp.int32, (1, NS), 1)
    return (jnp.minimum(sample + HALF, NS - 1) - jnp.maximum(sample - HALF, 0) + 1).astype(F32)


def fill_band(band):
    source = lax.broadcasted_iota(jnp.int32, band.shape, 0) - REACH
    target = lax.broadcasted_iota(jnp.int32, band.shape, 1)
    band[...] = jnp.where(jnp.abs(source - target) <= HALF, 1.0, 0.0).astype(BF16)


def fill_dft(dft):
    bins = K0 + lax.broadcasted_iota(jnp.int32, (PAD, 128), 0)
    sample = lax.broadcasted_iota(jnp.int32, (PAD, 128), 1)
    turn = 2.0 * math.pi / NS
    phase = ((bins * sample) & (NS - 1)).astype(F32) * turn
    step = ((bins * 128) & (NS - 1)).astype(F32) * turn
    cos, sin = jnp.cos(phase), jnp.sin(phase)
    step_cos, step_sin = jnp.cos(step), jnp.sin(step)
    scale = window_counts() * (1.0 / math.sqrt(NS))
    for tile in range(NS // 128):
        place = slice(tile * 128, (tile + 1) * 128)
        for part, value in enumerate((cos * scale[:, place], -sin * scale[:, place])):
            high = value.astype(BF16)
            dft[part * PAD : (part + 1) * PAD, place] = high
            dft[(2 + part) * PAD : (3 + part) * PAD, place] = (value - high.astype(F32)).astype(BF16)
        cos, sin = cos * step_cos - sin * step_sin, sin * step_cos + cos * step_sin


def front_kernel(x_hbm, x_ref, power_ref, band, dft, arrived):
    parts = arrived.shape[0]
    size = x_hbm.shape[0] // parts
    copies = [
        pltpu.make_async_copy(
            x_hbm.at[pl.ds(part * size, size)], x_ref.at[pl.ds(part * size, size)], arrived.at[part]
        )
        for part in range(parts)
    ]
    for copy in copies:
        copy.start()
    fill_band(band)
    fill_dft(dft)
    total = jnp.zeros((W, 128), F32)
    for part, copy in enumerate(copies):
        copy.wait()
        for channel in range(part * size, (part + 1) * size):
            for tile in range(NS // 128):
                value = x_ref[channel, :, tile * 128 : (tile + 1) * 128].astype(F32)
                total = total + value * value
    row = jnp.sum(jnp.transpose(total), axis=0, keepdims=True)
    power_ref[...] = jnp.concatenate([row, row], axis=1)


def front(strain_rate, parts=8):
    return pl.pallas_call(
        front_kernel,
        in_specs=[pl.BlockSpec(memory_space=pltpu.HBM)],
        out_specs=in_vmem(4),
        out_shape=[
            jax.ShapeDtypeStruct(strain_rate.shape, BF16),
            jax.ShapeDtypeStruct((1, LANES), F32),
            jax.ShapeDtypeStruct((TILE + 2 * REACH, TILE), BF16),
            jax.ShapeDtypeStruct((4 * PAD, NS), BF16),
        ],
        scratch_shapes=[pltpu.SemaphoreType.DMA((math.gcd(parts, strain_rate.shape[0]),))],
        compiler_params=pltpu.CompilerParams(vmem_limit_bytes=51 * 2**20),
        name="front",
    )(strain_rate)


def spectra_kernel(block, x_ref, band, dft, out_ref, rows):
    channels = x_ref.shape[0]
    small = window_counts() * 1e-06
    first_half = lax.broadcasted_iota(jnp.int32, (FS, LANES), 1) < W
    contract_samples = (((1,), (1,)), ((), ()))
    units = [
        (channel, tile) for channel in range(0, channels, block) for tile in range(NS // TILE)
    ]

    def running_sum(channel, tile):
        start, stop = tile * TILE, (tile + 1) * TILE
        low, high = max(start - REACH, 0), min(stop + REACH, NS)
        skip = low - (start - REACH)
        magnitude = jnp.abs(x_ref[channel : channel + block, :, low:high].reshape(-1, high - low))
        return jnp.dot(
            magnitude, band[skip : skip + high - low, :], preferred_element_type=F32
        )

    def flatten(channel, tile, running):
        start, stop = tile * TILE, (tile + 1) * TILE
        x = x_ref[channel : channel + block, :, start:stop].reshape(-1, TILE).astype(F32)
        flat = x / (running + small[:, start:stop])
        high = flat.astype(BF16)
        return high, (flat - high.astype(F32)).astype(BF16)

    def transform(tile, high, low):
        place = slice(tile * TILE, (tile + 1) * TILE)
        both = lax.dot_general(
            dft[:, place], high, contract_samples, preferred_element_type=F32
        )
        rest = lax.dot_general(
            dft[: 2 * PAD, place], low, contract_samples, preferred_element_type=F32
        )
        return both[: 2 * PAD] + (both[2 * PAD :] + rest)

    def store(channel, spectrum):
        white_real, white_imag = whiten_rows(spectrum)
        for pair in range(block // 2):
            real = white_real[:, pair * LANES : (pair + 1) * LANES]
            imag = white_imag[:, pair * LANES : (pair + 1) * LANES]
            even = jnp.where(first_half, real, pltpu.roll(imag, W, 1))
            odd = jnp.where(first_half, pltpu.roll(real, W, 1), imag)
            for bin_number in range(FS):
                for offset, value in enumerate((even, odd)):
                    row = channel + 2 * pair + offset
                    rows[bin_number, row : row + 1, :] = value[bin_number : bin_number + 1]

    summed, flattened = {}, {}
    for index in range(len(units) + 2):
        if index < len(units):
            summed[index] = running_sum(*units[index])
        if 1 <= index <= len(units):
            flattened[index - 1] = flatten(*units[index - 1], summed.pop(index - 1))
        if index >= 2:
            channel, tile = units[index - 2]
            term = transform(tile, *flattened.pop(index - 2))
            spectrum = term if tile == 0 else spectrum + term
            if tile == NS // TILE - 1:
                store(channel, spectrum)
    out_ref[...] = rows[...].astype(BF16)


def local_spectra(strain_rate, band, dft, block=8):
    channels = strain_rate.shape[0]
    return pl.pallas_call(
        functools.partial(spectra_kernel, block),
        in_specs=in_vmem(3),
        out_specs=in_vmem(1)[0],
        out_shape=jax.ShapeDtypeStruct((FS, channels, LANES), BF16),
        scratch_shapes=[pltpu.VMEM((FS, channels, LANES), F32)],
        compiler_params=pltpu.CompilerParams(vmem_limit_bytes=24 * 2**20),
        name="spectra",
    )(strain_rate, band, dft)


def message_kernel(spectra_ref, own_ref, *refs):
    *power_refs, out_ref = refs
    rows = spectra_ref.shape[0] * spectra_ref.shape[1]
    power = own_ref[...]
    for ref in power_refs:
        power = power + ref[...]
    power = jnp.broadcast_to(power, (8, LANES))
    high = power.astype(BF16)
    rest = power - high.astype(F32)
    middle = rest.astype(BF16)
    low = (rest - middle.astype(F32)).astype(BF16)
    line = lax.broadcasted_iota(jnp.int32, power.shape, 0)
    parts = jnp.where(
        line == 0, high.astype(F32), jnp.where(line == 1, middle.astype(F32), low.astype(F32))
    )
    power_rows = jnp.concatenate([parts, parts], axis=0).astype(BF16)
    spectra = spectra_ref[...].reshape(rows, LANES)
    for receiver in range(out_ref.shape[0]):
        out_ref[receiver, :rows, :] = spectra
        out_ref[receiver, rows:, :] = power_rows


def cross_kernel(order, members, samples, gathered_ref, own_ref, *refs):
    *row_refs, out_hbm, second, out_ref, sent = refs
    channels = own_ref.shape[1]
    rows = FS * channels
    power = None
    for block in range(len(order)):
        parts = gathered_ref[block, rows : rows + POWER_ROWS, :].astype(F32)
        value = parts[0:1] + (parts[1:2] + parts[2:3])
        power = value if power is None else power + value
    power = power / (channels * members * samples)
    gain_square = 1.0 / (power + 1e-05)
    lane = lax.broadcasted_iota(jnp.int32, (1, LANES), 1)
    turned_gain = jnp.where(lane < W, -gain_square, gain_square)
    me = lax.axis_index("row")
    copies = []
    for bin_number in range(FS):
        for shift, ref in enumerate((own_ref, *row_refs)):
            row = jnp.bitwise_xor(me, shift)
            place = pl.ds(pl.multiple_of(row * channels, channels), channels)
            value = ref[bin_number].astype(F32)
            second[bin_number, 0, place, :] = (value * gain_square).astype(BF16)
            second[bin_number, 1, place, :] = (pltpu.roll(value, W, 1) * turned_gain).astype(BF16)
        first = jnp.concatenate(
            [
                gathered_ref[order.index(column), bin_number * channels : (bin_number + 1) * channels, :]
                for column in range(len(order))
            ],
            axis=0,
        )
        total = lax.dot_general(
            second[bin_number].reshape(-1, LANES),
            first,
            (((1,), (1,)), ((), ())),
            preferred_element_type=F32,
        )
        out_ref[bin_number] = (total * (1.0 / W)).astype(BF16).reshape(out_ref.shape[1:])
        copy = pltpu.make_async_copy(
            out_ref.at[bin_number], out_hbm.at[:, bin_number], sent.at[bin_number]
        )
        copy.start()
        copies.append(copy)
    for copy in copies:
        copy.wait()


def column_order(col_count):
    best = [4, 2, 3, 6, 5, 1, 0, 7]
    if col_count == len(best):
        return best
    middle = col_count // 2
    return [middle, *(c for c in range(col_count) if c != middle)]


def shards(strain_rate):
    channels, windows, samples = strain_rate.shape
    row_count = lax.axis_size("row")
    col_count = lax.axis_size("col")
    order = column_order(col_count)

    def from_row(value, shift):
        return lax.ppermute(value, "row", [(i, i ^ shift) for i in range(row_count)])

    held, own_power, band, dft = front(strain_rate)
    powers = [from_row(own_power, shift) for shift in range(1, row_count)]
    spectra = local_spectra(held, band, dft)
    message = pl.pallas_call(
        message_kernel,
        in_specs=in_vmem(1 + row_count),
        out_specs=in_vmem(1)[0],
        out_shape=jax.ShapeDtypeStruct((col_count, FS * channels + POWER_ROWS, LANES), BF16),
        compiler_params=pltpu.CompilerParams(vmem_limit_bytes=8 * 2**20),
        name="message",
    )(spectra, own_power, *powers)
    gathered = lax.all_to_all(message, "col", 0, 0, axis_index_groups=[order])
    others = [from_row(spectra, shift) for shift in range(1, row_count)]
    result = pl.pallas_call(
        functools.partial(cross_kernel, order, row_count * col_count, samples),
        in_specs=in_vmem(2 + len(others)),
        out_specs=pl.BlockSpec(memory_space=pltpu.HBM),
        out_shape=jax.ShapeDtypeStruct(
            (2, FS, row_count * channels, col_count * channels), BF16
        ),
        scratch_shapes=[
            pltpu.VMEM((FS, 2, row_count * channels, LANES), BF16),
            pltpu.VMEM((FS, 2, row_count * channels, col_count * channels), BF16),
            pltpu.SemaphoreType.DMA((FS,)),
        ],
        compiler_params=pltpu.CompilerParams(vmem_limit_bytes=8 * 2**20),
        name="cross",
    )(gathered, spectra, *others)
    return result.reshape(2, FS, 1, row_count, channels, -1)


def solution(mesh):
    return jax.shard_map(
        shards,
        mesh=mesh,
        in_specs=(P(("row", "col"), None, None),),
        out_specs=P(None, None, "col", None, None, "row"),
        check_vma=False,
    )
```
